32 devices in a mesh: src: 8 (over z, y), dst: 4 (over x, core).
Axes of the slice: x: 2, y: 2, z: 4, core: 2. Of those that a mesh axis runs over, the one named last changes fastest.
Arguments:
- transition: bfloat16 [16384, 16384], P('src', 'dst'), may hold values from 5.4931641e-06 to 0.05
- emission: bfloat16 [8192, 16384], P('src', 'dst'), may hold values from 0.099609375 to 5
- forward: bfloat16 [3, 256, 16384], P(None, None, 'src'), may hold values from 0.25 to 4
- beta_end: bfloat16 [256, 16384], P(None, 'dst'), may hold values from 0.5 to 2
- scales: float32 [3, 256], replicated, may hold values from 0.5 to 2
- tokens: int32 [3, 256], replicated, may hold values from 0 to 8191
Outputs:
- counts: float32 [16384, 16384], P('src', 'dst')
- beta_first: float32 [256, 16384], P('dst', 'src')
The draws below stay inside these ranges and needn't reach their ends.
All inputs are finite; a program needn't handle non-finite values.
Results may differ from the reference program's by a relative error of at most 0.00076.
Values may be sent and summed in bfloat16 or wider, within the bound.
No kernel may reach another device: no remote copies, remote signals or barrier semaphores. Data moves between devices by JAX's collectives and lax.ppermute only.
A program may use at most 192 MiB of HBM per device.

```python
import math
import jax
import jax.numpy as jnp
from jax import lax

S = 16384
V = 8192
B = 256
STEPS = 3


def draw_transition(key, part):
    first_key = jax.random.fold_in(key, 11)
    second_key = jax.random.fold_in(key, 23)
    third_key = jax.random.fold_in(key, 37)
    hits = jax.random.randint(second_key, (S, S), 0, S) < 32
    base = jnp.exp(jax.random.uniform(first_key, (S, S), jnp.float32, math.log(0.1), math.log(1.0))) / S
    spike = jnp.exp(jax.random.uniform(third_key, (S, S), jnp.float32, math.log(0.005), math.log(0.049)))
    return jnp.where(hits, spike, base).astype(jnp.bfloat16)


def place_ends(result, key, low, high):
    spot = [jax.random.randint(jax.random.fold_in(key, axis), (), 0, length) for axis, length in enumerate(result.shape)]
    main_axis = result.shape.index(max(result.shape))
    next_to = spot[:main_axis] + [(spot[main_axis] + 1) % result.shape[main_axis]] + spot[main_axis + 1:]
    return result.at[tuple(spot)].set(low).at[tuple(next_to)].set(high)


def level_of(own_key, extent, pieces, low, top_value):
    def one(position, parts):
        heights = jax.random.uniform(jax.random.fold_in(jax.random.fold_in(own_key, 6), position), (parts,), jnp.float32, low / len(pieces), top_value / len(pieces))
        return jnp.repeat(jnp.exp(heights), extent[position] // parts).reshape((-1,) + (1,) * (len(extent) - position - 1))

    loudness = one(*pieces[0])
    for cut in pieces[1:]:
        loudness = loudness * one(*cut)
    return loudness


def setup_inputs(seed: int = 0) -> dict:
    splits = jax.random.split(jax.random.key(seed), 7)
    transition = draw_transition(jax.random.fold_in(splits[6], 71), 0)
    emission = jnp.clip(jnp.exp(math.log(5.0) - 3.915937 * jax.random.uniform(splits[1], (V, S), jnp.float32) ** level_of(splits[1], (V, S), ((0, 8), (1, 4)), -0.2, 0.2)), 0.099609375, 5.0).astype(jnp.bfloat16)
    forward = jnp.clip(jnp.exp(math.log(4.0) - 2.7725887 * jax.random.uniform(splits[2], (STEPS, B, S), jnp.float32) ** level_of(splits[2], (STEPS, B, S), ((2, 8),), -0.2, 0.2)), 0.25, 4.0).astype(jnp.bfloat16)
    beta_end = jnp.clip(jnp.exp(math.log(2.0) - 1.3862944 * jax.random.uniform(splits[3], (B, S), jnp.float32) ** level_of(splits[3], (B, S), ((1, 4),), -0.2, 0.2)), 0.5, 2.0).astype(jnp.bfloat16)
    scales = jnp.clip(jnp.exp(jax.random.uniform(splits[4], (STEPS, B), jnp.float32, math.log(0.5), math.log(2.0))), 0.5, 2.0)
    tokens = place_ends(jax.random.randint(splits[5], (STEPS, B), 0, V), jax.random.fold_in(splits[5], 1), 0, V - 1).astype(jnp.int32)
    return dict(transition=transition, emission=emission, forward=forward, beta_end=beta_end, scales=scales, tokens=tokens)


def reference(transition, emission, forward, beta_end, scales, tokens):
    message = beta_end
    weights = []
    summed = jnp.zeros((B, S), jnp.float32)
    for step in range(STEPS - 1, -1, -1):
        emitted = emission[tokens[step].astype(jnp.int32)]
        weighted = (emitted.astype(jnp.float32) * message.astype(jnp.float32) / scales[step][:, None]).astype(jnp.bfloat16)
        weights.insert(0, weighted)
        summed = lax.dot_general(weighted, transition, (((1,), (1,)), ((), ())), preferred_element_type=jnp.float32)
        message = summed.astype(jnp.bfloat16)
    stacked = jnp.stack(weights, axis=0).reshape(STEPS * B, S)
    pairs = lax.dot_general(forward.reshape(STEPS * B, S), stacked, (((0,), (0,)), ((), ())), preferred_element_type=jnp.float32)
    counts = transition.astype(jnp.float32) * pairs * (32.0 / (STEPS * B))
    return counts, summed
```

```python
import functools

import jax
import jax.numpy as jnp
import numpy as np
from jax import lax
from jax.experimental import pallas as pl
from jax.experimental.pallas import tpu as pltpu
from jax.sharding import PartitionSpec as P

F32 = jnp.float32
BF16 = jnp.bfloat16
VMEM_LIMIT = 60 * 1024 * 1024


def local_rows(words, emission, first_word):
    keys = words - first_word
    table = (keys[:, None] == jnp.arange(emission.shape[0], dtype=jnp.int32)[None, :]).astype(BF16)
    return jnp.dot(table, emission, preferred_element_type=BF16)


def dense_plan(transition, emission, forward, beta_end, scales, tokens):
    steps, batch, _ = forward.shape
    src_cols, dst_cols = transition.shape
    share = batch // lax.axis_size("dst")
    first_word = lax.axis_index("src") * emission.shape[0]
    rows = local_rows(tokens.reshape(-1), emission, first_word)
    emitted_all = lax.psum(rows, "src").astype(F32).astype(BF16).reshape(steps, batch, dst_cols)
    message = beta_end
    pairs = jnp.zeros((src_cols, dst_cols), F32)
    beta_first = jnp.zeros((share, src_cols), F32)
    for step in range(steps - 1, -1, -1):
        weighted = (
            emitted_all[step].astype(F32) * message.astype(F32) / scales[step][:, None]
        ).astype(BF16)
        pairs = pairs + lax.dot_general(
            forward[step], weighted, (((0,), (0,)), ((), ())), preferred_element_type=F32
        )
        partial_rows = lax.dot_general(
            weighted, transition, (((1,), (1,)), ((), ())), preferred_element_type=F32
        )
        shares = lax.psum_scatter(partial_rows, "dst", scatter_dimension=0, tiled=True)
        if step == 0:
            beta_first = shares
        else:
            whole_rows = lax.all_gather(shares.astype(BF16), "src", axis=1, tiled=True)
            message = lax.all_to_all(whole_rows, "dst", split_axis=1, concat_axis=0, tiled=True)
    counts = transition.astype(F32) * pairs * (32.0 / (steps * batch))
    return counts, beta_first


def ring_order(n):
    return list(range(0, n, 2)) + list(range(n - 1, 0, -2))


def ring_tables(n):
    ring = ring_order(n)
    origin = np.zeros((n, n), np.int32)
    for at, s in enumerate(ring):
        places = [s]
        for hop in range(1, n // 2 + 1):
            places.append(ring[(at - hop) % n])
            if hop < n - n // 2:
                places.append(ring[(at + hop) % n])
        origin[s] = places
    return origin


def ring_gather(piece, n, beside=None):
    ring = ring_order(n)
    ahead = [(ring[i], ring[(i + 1) % n]) for i in range(n)]
    behind = [(b, a) for a, b in ahead]
    out, f, b, done = [piece], piece, piece, None
    for hop in range(1, n // 2 + 1):
        if done is not None:
            f, b, done = lax.optimization_barrier((f, b, done))
        if beside is not None:
            done = beside(hop, out, done)
        f = lax.ppermute(f, "src", ahead)
        new = [f]
        if hop < n - n // 2:
            b = lax.ppermute(b, "src", behind)
            new.append(b)
        out = out + new
    return out, done


def params(flops, nbytes):
    return dict(
        compiler_params=pltpu.CompilerParams(vmem_limit_bytes=VMEM_LIMIT),
        cost_estimate=pl.CostEstimate(flops=flops, bytes_accessed=nbytes, transcendentals=0),
    )


def dot_nt(a, b):
    return lax.dot_general(a, b, (((1,), (1,)), ((), ())), preferred_element_type=F32)


def product(meta, weights, width, transition, tiles, tile, row_tile, init=None, out_dtype=F32):
    n = len(weights)
    batch = weights[0][0].shape[0]

    def kernel(meta_ref, *refs):
        ws, ts = refs[:n], refs[n : 2 * n]
        acc = refs[2 * n][...] if init is not None else None
        out = refs[-1]
        for w, t in zip(ws, ts):
            d = dot_nt(w[...], t[...])
            acc = d if acc is None else acc + d
        out[...] = acc.astype(out.dtype)

    in_specs = [
        pl.BlockSpec((batch, width), functools.partial(lambda at, i, m: (0, at), at)) for _, at, _ in weights
    ] + [
        pl.BlockSpec((tile, width), functools.partial(lambda col, i, m: (row_tile(i, m), col(m)), col))
        for _, _, col in weights
    ]
    args = [w for w, _, _ in weights] + [transition] * n
    if init is not None:
        in_specs.append(pl.BlockSpec((batch, tile), lambda i, m: (0, row_tile(i, m))))
        args.append(init)
    rows = tiles * tile
    return pl.pallas_call(
        kernel,
        grid_spec=pltpu.PrefetchScalarGridSpec(
            num_scalar_prefetch=1,
            grid=(tiles,),
            in_specs=in_specs,
            out_specs=pl.BlockSpec((batch, tile), lambda i, m: (0, i)),
        ),
        out_shape=jax.ShapeDtypeStruct((batch, rows), out_dtype),
        **params(2 * batch * rows * width * n, 2 * width * n * (rows + batch) + 4 * batch * rows),
    )(meta, *args)


def split_product(meta, weights, width, transition, init, n_x, tile, core_at):
    n = len(weights)
    batch = weights[0][0].shape[0]
    rows = transition.shape[0]
    share = batch // (2 * n_x)

    def kernel(meta_ref, *refs):
        ws, ts = refs[:n], refs[n : 2 * n]
        start, theirs, own, whole = refs[2 * n :]
        acc = start[...]
        for w, t in zip(ws, ts):
            acc = acc + dot_nt(w[...], t[...])
        whole[...] = acc
        core = meta_ref[core_at]
        for x in range(n_x):
            here = pl.ds(x * share, share)
            theirs[here, :] = whole[pl.ds(pl.multiple_of((2 * x + 1 - core) * share, 8), share), :]
            own[here, :] = whole[pl.ds(pl.multiple_of((2 * x + core) * share, 8), share), :]

    in_specs = (
        [pl.BlockSpec((batch, width), lambda i, m: (0, 0))] * n
        + [
            pl.BlockSpec((tile, width), functools.partial(lambda col, i, m: (i, col(m)), col))
            for _, _, col in weights
        ]
        + [pl.BlockSpec((batch, tile), lambda i, m: (0, i))]
    )
    half = jax.ShapeDtypeStruct((batch // 2, rows), F32)
    return pl.pallas_call(
        kernel,
        grid_spec=pltpu.PrefetchScalarGridSpec(
            num_scalar_prefetch=1,
            grid=(rows // tile,),
            in_specs=in_specs,
            out_specs=[pl.BlockSpec((batch // 2, tile), lambda i, m: (0, i))] * 2,
            scratch_shapes=[pltpu.VMEM((batch, tile), F32)],
        ),
        out_shape=[half, half],
        **params(2 * batch * rows * width * n, 2 * width * n * (rows + batch) + 8 * batch * rows),
    )(meta, *[w for w, _, _ in weights], *([transition] * n), init)


def compact_rows(slot_words, emission, cap_a, width):
    slots = slot_words.shape[0]
    words, cols = emission.shape

    def kernel(w_ref, e_ref, a_ref, b_ref):
        ids = lax.broadcasted_iota(jnp.int32, (slots, words), 1)
        table = jnp.where(w_ref[...] == ids, 1.0, 0.0).astype(BF16)
        rows = jnp.dot(table, e_ref[...], preferred_element_type=F32).astype(BF16)
        a_ref[...] = rows[:cap_a]
        b_ref[...] = rows[cap_a:]

    return pl.pallas_call(
        kernel,
        grid=(cols // width,),
        in_specs=[
            pl.BlockSpec((slots, 1), lambda i: (0, 0)),
            pl.BlockSpec((words, width), lambda i: (0, i)),
        ],
        out_specs=[
            pl.BlockSpec((cap_a, width), lambda i: (0, i)),
            pl.BlockSpec((slots - cap_a, width), lambda i: (0, i)),
        ],
        out_shape=[
            jax.ShapeDtypeStruct((cap_a, cols), BF16),
            jax.ShapeDtypeStruct((slots - cap_a, cols), BF16),
        ],
        **params(2 * slots * words * cols, 2 * words * cols),
    )(slot_words[:, None], emission)


def expand(places, pieces, beta_end, scale, width):
    n = len(pieces)
    cap, cols = pieces[0].shape
    batch = beta_end.shape[0]

    def kernel(e_ref, b_ref, s_ref, *refs):
        out = refs[n]
        slots = jnp.concatenate([r[...] for r in refs[:n]], axis=0)
        emitted = jnp.dot(e_ref[...], slots, preferred_element_type=F32)
        out[...] = (emitted * b_ref[...].astype(F32) / s_ref[...]).astype(BF16)

    return pl.pallas_call(
        kernel,
        grid=(cols // width,),
        in_specs=[
            pl.BlockSpec((batch, n * cap), lambda i: (0, 0)),
            pl.BlockSpec((batch, width), lambda i: (0, i)),
            pl.BlockSpec((batch, 1), lambda i: (0, 0)),
        ]
        + [pl.BlockSpec((cap, width), lambda i: (0, i))] * n,
        out_specs=pl.BlockSpec((batch, width), lambda i: (0, i)),
        out_shape=jax.ShapeDtypeStruct((batch, cols), BF16),
        **params(2 * batch * n * cap * cols, 2 * cols * (n * cap + 2 * batch)),
    )(places, beta_end, scale, *pieces)


def counts_chunks(meta, forward, chunks, last, places, transition, counts, factor, tile):
    rows, depth = forward.shape
    n, steps = len(places), len(chunks[0]) + 1
    batch, width = chunks[0][0].shape

    def at(p, m):
        out = m[places[-1]]
        for k in range(n - 1):
            out = jnp.where(p == k, m[places[k]], out)
        return out

    whole = pl.BlockSpec((batch, width), lambda p, i, m: (0, 0))
    in_specs = [
        pl.BlockSpec((tile, depth), lambda p, i, m: (i, 0)),
        pl.BlockSpec((tile, width), lambda p, i, m: (i, at(p, m))),
        pl.BlockSpec((batch, width), lambda p, i, m: (0, at(p, m))),
    ] + [whole] * (n * (steps - 1))

    def kernel(meta_ref, f_ref, t_ref, last_ref, *refs):
        out, stacked = refs[-2:]
        for k in range(n):

            @pl.when((pl.program_id(0) == k) & (pl.program_id(1) == 0))
            def _(k=k):
                for step in range(steps - 1):
                    stacked[pl.ds(step * batch, batch), :] = refs[k * (steps - 1) + step][...]
                stacked[pl.ds((steps - 1) * batch, batch), :] = last_ref[...]

        pairs = jnp.dot(f_ref[...], stacked[...], preferred_element_type=F32)
        out[...] = t_ref[...].astype(F32) * pairs * factor

    args = [forward, transition, last] + [w for chunk in chunks for w in chunk]
    aliases = {}
    if counts is not None:
        in_specs.append(pl.BlockSpec(memory_space=pl.ANY))
        args.append(counts)
        aliases = {len(args): 0}
    return pl.pallas_call(
        kernel,
        grid_spec=pltpu.PrefetchScalarGridSpec(
            num_scalar_prefetch=1,
            grid=(n, rows // tile),
            in_specs=in_specs,
            out_specs=pl.BlockSpec((tile, width), lambda p, i, m: (i, at(p, m))),
            scratch_shapes=[pltpu.VMEM((depth, width), BF16)],
        ),
        out_shape=jax.ShapeDtypeStruct(transition.shape, F32),
        input_output_aliases=aliases,
        **params(2 * rows * depth * width * n, n * (rows * width * 6 + 2 * depth * (rows + width))),
    )(meta, *args)


def capacity(rows, n_src):
    mean = rows // n_src
    return -(-(3 * mean) // 32) * 16


def ranks(owner):
    n = owner.shape[0]
    same = owner[:, None] == owner[None, :]
    before = lax.broadcasted_iota(jnp.int32, (n, n), 1) < lax.broadcasted_iota(jnp.int32, (n, n), 0)
    return jnp.sum((same & before).astype(jnp.int32), axis=1)


def slot_plan(caps, transition, emission, forward, beta_end, scales, tokens):
    steps, batch, _ = forward.shape
    src_cols, dst_cols = transition.shape
    n_src, n_dst = lax.axis_size("src"), lax.axis_size("dst")
    n_x, ratio = n_dst // 2, n_src // n_dst
    width = dst_cols // n_src
    words = emission.shape[0]
    s, d = lax.axis_index("src"), lax.axis_index("dst")
    x, core = d // 2, lax.rem(d, 2)
    share = batch // n_dst

    owner = tokens // words
    local = tokens - owner * words
    rest = steps - 1
    cap_a, cap_b = caps
    rank_a = ranks(owner[rest])
    rank_b = ranks(owner[:rest].reshape(-1))

    def word_of_slot(rank, own, loc, cap):
        hit = (rank[None, :] == jnp.arange(cap, dtype=jnp.int32)[:, None]) & (own == s)[None, :]
        return jnp.sum(jnp.where(hit, loc[None, :] + 1, 0), axis=1) - 1

    slot_words = jnp.concatenate(
        [
            word_of_slot(rank_a, owner[rest], local[rest], cap_a),
            word_of_slot(rank_b, owner[:rest].reshape(-1), local[:rest].reshape(-1), cap_b),
        ]
    )
    compact_a, compact_b = compact_rows(slot_words, emission, cap_a, dst_cols // 4)

    origin = jnp.asarray(ring_tables(n_src))[s]
    ids = (origin[:, None] * cap_a + jnp.arange(cap_a, dtype=jnp.int32)[None, :]).reshape(-1)
    places_a = ((owner[rest] * cap_a + rank_a)[:, None] == ids[None, :]).astype(BF16)
    slots_a, _ = ring_gather(compact_a, n_src)
    last = expand(places_a, slots_a, beta_end, scales[rest][:, None], dst_cols // 4)

    compact_b, _ = lax.optimization_barrier((compact_b, slots_a[-1]))
    by_chunk = compact_b.reshape(cap_b, ratio, n_dst, width).transpose(2, 1, 0, 3)
    got = lax.all_to_all(by_chunk.reshape(n_src, cap_b, width), "src", 0, 0).reshape(n_src * cap_b, width)
    slot_b = owner[:rest].reshape(-1) * cap_b + rank_b
    places_b = (slot_b[:, None] == jnp.arange(n_src * cap_b, dtype=jnp.int32)[None, :]).astype(BF16)
    emitted = jnp.dot(places_b, got, preferred_element_type=BF16).reshape(rest, batch, width)

    to_core = [(t, t ^ 1) for t in range(n_dst)]
    to_x = [(t, (t + 2) % n_dst) for t in range(n_dst)]
    to_part = []
    for a in range(n_src):
        for t in range(n_dst):
            e = (t % 2) * n_x + t // 2
            to_part.append((a * n_dst + t, (e * ratio + a % ratio) * n_dst + a // ratio))

    cols = lax.rem(origin, ratio) * n_dst + origin // ratio
    meta = jnp.concatenate([cols, jnp.stack([core, x]).astype(jnp.int32)])
    core_at, x_at = n_src, n_src + 1
    factor = 32.0 / (steps * batch)
    flat = forward.reshape(steps * batch, src_cols).T
    tiles = src_cols // width

    def from_meta(p):
        return lambda m: m[p]

    def fixed(p):
        return lambda m: p

    def part(h, m):
        return lax.rem(m[x_at] + n_x - 1 - h, n_x)

    def row_there(h, m):
        return (1 - m[core_at]) * n_x + part(h, m)

    def row_here(h, m):
        return m[core_at] * n_x + part(h, m)

    def gathered(pieces, places):
        return [(pieces[p], 0, from_meta(p)) for p in places]

    def between(hop, pieces, done):
        init, counts = done if done is not None else (None, None)
        if hop == 1:
            if len(held) == rest - 1:
                counts = counts_of([0], pieces, counts)
            return init, counts
        new = range(0, 3) if hop == 2 else range(2 * hop - 3, 2 * hop - 1)
        init = product(
            meta, gathered(pieces, new), width, transition, tiles // 2, 2 * width, lambda i, m: i, init
        )
        return init, counts

    def counts_of(places, pieces, counts):
        chunks = [[pieces[p]] + [h[p] for h in held[::-1]] for p in places]
        return counts_chunks(meta, flat, chunks, last, places, transition, counts, factor, src_cols)

    weights, init = [(last, p, fixed(p)) for p in range(n_src)], None
    held = []
    for step in range(rest, 0, -1):
        theirs = product(meta, weights, width, transition, n_x, width, row_there, init)
        theirs = lax.ppermute(theirs, "dst", to_core)
        own = product(meta, weights, width, transition, n_x, width, row_here, init)
        total = None
        for h in range(n_x):
            at = slice(h * width, (h + 1) * width)
            term = own[:, at] + theirs[:, at]
            if total is not None:
                term = term + lax.ppermute(total, "dst", to_x).astype(F32)
            total = term.astype(BF16)
        message = lax.ppermute(total, ("src", "dst"), to_part)
        mine = (
            emitted[step - 1].astype(F32) * message.astype(F32) / scales[step - 1][:, None]
        ).astype(BF16)
        pieces, (init, counts) = ring_gather(mine, n_src, between)
        held.append(pieces)
        weights = gathered(pieces, [n_src - 1])

    theirs, own = split_product(meta, weights, width, transition, init, n_x, 2 * width, core_at)
    both = own + lax.ppermute(theirs, "dst", to_core)
    total = None
    for h in range(n_x):
        k = lax.rem(x + n_x - 1 - h, n_x)
        term = lax.dynamic_slice_in_dim(both, k * share, share, 0)
        total = term if total is None else term + lax.ppermute(total, "dst", to_x)
    pieces = held.pop()
    counts = counts_of(list(range(1, n_src)), pieces, counts)
    return counts, total


def per_device(transition, emission, forward, beta_end, scales, tokens):
    steps, batch, _ = forward.shape
    n_src, n_dst = lax.axis_size("src"), lax.axis_size("dst")
    width = transition.shape[1] // n_src
    args = (transition, emission, forward, beta_end, scales, tokens)
    fits = (
        n_src % n_dst == 0
        and n_src & (n_src - 1) == 0
        and n_dst % 2 == 0
        and width % 256 == 0
        and steps > 1
        and (batch // n_dst) % 16 == 0
    )
    if not fits:
        return dense_plan(*args)
    owner = tokens // emission.shape[0]
    held = jnp.sum((owner[:, :, None] == jnp.arange(n_src, dtype=jnp.int32)).astype(jnp.int32), axis=1)
    last, others = held[steps - 1], jnp.sum(held[: steps - 1], axis=0)
    caps = capacity(batch, n_src), capacity((steps - 1) * batch, n_src)
    room = (jnp.max(last) <= caps[0]) & (jnp.max(others) <= caps[1])
    every = batch, (steps - 1) * batch
    return lax.cond(
        room, functools.partial(slot_plan, caps), functools.partial(slot_plan, every), *args
    )


def solution(mesh):
    in_specs = (P("src", "dst"), P("src", "dst"), P(None, None, "src"), P(None, "dst"), P(), P())
    out_specs = (P("src", "dst"), P("dst", "src"))
    return jax.shard_map(
        per_device, mesh=mesh, in_specs=in_specs, out_specs=out_specs, check_vma=False
    )
```

```python
import functools

import jax
import jax.numpy as jnp
import numpy as np
from jax import lax
from jax.experimental import pallas as pl
from jax.experimental.pallas import tpu as pltpu
from jax.sharding import PartitionSpec as P

F32 = jnp.float32
BF16 = jnp.bfloat16
MIB = 1024 * 1024
PRODUCT = 24 * MIB
COUNTS = 63 * MIB


def local_rows(words, emission, first_word):
    keys = words - first_word
    table = (keys[:, None] == jnp.arange(emission.shape[0], dtype=jnp.int32)[None, :]).astype(BF16)
    return jnp.dot(table, emission, preferred_element_type=BF16)


def dense_plan(transition, emission, forward, beta_end, scales, tokens):
    steps, batch, _ = forward.shape
    src_cols, dst_cols = transition.shape
    share = batch // lax.axis_size("dst")
    first_word = lax.axis_index("src") * emission.shape[0]
    rows = local_rows(tokens.reshape(-1), emission, first_word)
    emitted_all = lax.psum(rows, "src").astype(F32).astype(BF16).reshape(steps, batch, dst_cols)
    message = beta_end
    pairs = jnp.zeros((src_cols, dst_cols), F32)
    beta_first = jnp.zeros((share, src_cols), F32)
    for step in range(steps - 1, -1, -1):
        weighted = (
            emitted_all[step].astype(F32) * message.astype(F32) / scales[step][:, None]
        ).astype(BF16)
        pairs = pairs + lax.dot_general(
            forward[step], weighted, (((0,), (0,)), ((), ())), preferred_element_type=F32
        )
        partial_rows = lax.dot_general(
            weighted, transition, (((1,), (1,)), ((), ())), preferred_element_type=F32
        )
        shares = lax.psum_scatter(partial_rows, "dst", scatter_dimension=0, tiled=True)
        if step == 0:
            beta_first = shares
        else:
            whole_rows = lax.all_gather(shares.astype(BF16), "src", axis=1, tiled=True)
            message = lax.all_to_all(whole_rows, "dst", split_axis=1, concat_axis=0, tiled=True)
    counts = transition.astype(F32) * pairs * (32.0 / (steps * batch))
    return counts, beta_first


def ring_order(n):
    return list(range(0, n, 2)) + list(range(n - 1, 0, -2))


def ring_tables(n):
    ring = ring_order(n)
    origin = np.zeros((n, n), np.int32)
    for at, s in enumerate(ring):
        places = [s]
        for hop in range(1, n // 2 + 1):
            places.append(ring[(at - hop) % n])
            if hop < n - n // 2:
                places.append(ring[(at + hop) % n])
        origin[s] = places
    return origin


def ring_gather(piece, n, beside=None):
    ring = ring_order(n)
    ahead = [(ring[i], ring[(i + 1) % n]) for i in range(n)]
    behind = [(b, a) for a, b in ahead]
    out, f, b, done = [piece], piece, piece, None
    for hop in range(1, n // 2 + 1):
        if done is not None:
            f, b, done = lax.optimization_barrier((f, b, done))
        if beside is not None:
            done = beside(hop, out, done)
        f = lax.ppermute(f, "src", ahead)
        new = [f]
        if hop < n - n // 2:
            b = lax.ppermute(b, "src", behind)
            new.append(b)
        out = out + new
    return out, done


def params(flops, nbytes, vmem=63 * MIB):
    return dict(
        compiler_params=pltpu.CompilerParams(vmem_limit_bytes=vmem),
        cost_estimate=pl.CostEstimate(flops=flops, bytes_accessed=nbytes, transcendentals=0),
    )


def dot_nt(a, b):
    return lax.dot_general(a, b, (((1,), (1,)), ((), ())), preferred_element_type=F32)


def product(meta, weights, width, transition, tiles, tile, row_tile, init=None, out_dtype=F32):
    n = len(weights)
    batch = weights[0][0].shape[0]

    def kernel(meta_ref, *refs):
        ws, ts = refs[:n], refs[n : 2 * n]
        acc = refs[2 * n][...] if init is not None else None
        out = refs[-1]
        for w, t in zip(ws, ts):
            d = dot_nt(w[...], t[...])
            acc = d if acc is None else acc + d
        out[...] = acc.astype(out.dtype)

    in_specs = [
        pl.BlockSpec((batch, width), functools.partial(lambda at, i, m: (0, at), at)) for _, at, _ in weights
    ] + [
        pl.BlockSpec((tile, width), functools.partial(lambda col, i, m: (row_tile(i, m), col(m)), col))
        for _, _, col in weights
    ]
    args = [w for w, _, _ in weights] + [transition] * n
    if init is not None:
        in_specs.append(pl.BlockSpec((batch, tile), lambda i, m: (0, row_tile(i, m))))
        args.append(init)
    rows = tiles * tile
    return pl.pallas_call(
        kernel,
        grid_spec=pltpu.PrefetchScalarGridSpec(
            num_scalar_prefetch=1,
            grid=(tiles,),
            in_specs=in_specs,
            out_specs=pl.BlockSpec((batch, tile), lambda i, m: (0, i)),
        ),
        out_shape=jax.ShapeDtypeStruct((batch, rows), out_dtype),
        **params(2 * batch * rows * width * n, 2 * width * n * (rows + batch) + 4 * batch * rows, PRODUCT),
    )(meta, *args)


def split_product(meta, weights, width, transition, init, n_x, tile, core_at):
    n = len(weights)
    batch = weights[0][0].shape[0]
    rows = transition.shape[0]
    share = batch // (2 * n_x)

    def kernel(meta_ref, *refs):
        ws, ts = refs[:n], refs[n : 2 * n]
        start, theirs, own, whole = refs[2 * n :]
        acc = start[...]
        for w, t in zip(ws, ts):
            acc = acc + dot_nt(w[...], t[...])
        whole[...] = acc
        core = meta_ref[core_at]
        for x in range(n_x):
            here = pl.ds(x * share, share)
            theirs[here, :] = whole[pl.ds(pl.multiple_of((2 * x + 1 - core) * share, 8), share), :]
            own[here, :] = whole[pl.ds(pl.multiple_of((2 * x + core) * share, 8), share), :]

    in_specs = (
        [pl.BlockSpec((batch, width), lambda i, m: (0, 0))] * n
        + [
            pl.BlockSpec((tile, width), functools.partial(lambda col, i, m: (i, col(m)), col))
            for _, _, col in weights
        ]
        + [pl.BlockSpec((batch, tile), lambda i, m: (0, i))]
    )
    half = jax.ShapeDtypeStruct((batch // 2, rows), F32)
    return pl.pallas_call(
        kernel,
        grid_spec=pltpu.PrefetchScalarGridSpec(
            num_scalar_prefetch=1,
            grid=(rows // tile,),
            in_specs=in_specs,
            out_specs=[pl.BlockSpec((batch // 2, tile), lambda i, m: (0, i))] * 2,
            scratch_shapes=[pltpu.VMEM((batch, tile), F32)],
        ),
        out_shape=[half, half],
        **params(2 * batch * rows * width * n, 2 * width * n * (rows + batch) + 8 * batch * rows, PRODUCT),
    )(meta, *[w for w, _, _ in weights], *([transition] * n), init)


def compact_rows(slot_words, emission, caps, width, n_dst):
    words, cols = emission.shape
    slots = sum(caps)
    wide = 2 * width
    n = cols // wide
    half, across = n // 2, n_dst // 2

    def kernel(w_ref, e_ref, *refs):
        i = pl.program_id(0)
        ids = lax.broadcasted_iota(jnp.int32, (slots, words), 1)
        table = jnp.where(w_ref[...] == ids, 1.0, 0.0).astype(BF16)
        rows = jnp.dot(table, e_ref[...], preferred_element_type=F32).astype(BF16)

        @pl.when(i < half)
        def _():
            refs[0][...] = rows[: caps[0]]

        @pl.when(i >= half)
        def _():
            refs[1][...] = rows[: caps[0]]

        at = caps[0]
        for cap, ref in zip(caps[1:], refs[2:]):
            for k in range(2):
                ref[k, 0] = rows[at : at + cap, k * width : (k + 1) * width]
            at += cap

    return pl.pallas_call(
        kernel,
        grid=(n,),
        in_specs=[
            pl.BlockSpec((slots, 1), lambda i: (0, 0)),
            pl.BlockSpec((words, wide), lambda i: (0, i)),
        ],
        out_specs=[
            pl.BlockSpec((caps[0], wide), lambda i: (0, jnp.minimum(i, half - 1))),
            pl.BlockSpec((caps[0], wide), lambda i: (0, jnp.maximum(i - half, 0))),
        ]
        + [
            pl.BlockSpec((2, 1, cap, width), lambda i: (lax.rem(i, across), i // across, 0, 0))
            for cap in caps[1:]
        ],
        out_shape=[jax.ShapeDtypeStruct((caps[0], cols // 2), BF16)] * 2
        + [jax.ShapeDtypeStruct((n_dst, cols // width // n_dst, cap, width), BF16) for cap in caps[1:]],
        **params(2 * slots * words * cols, 2 * words * cols),
    )(slot_words[:, None], emission)


def ring_gather_halves(pieces, n, beside):
    ring = ring_order(n)
    ahead = [(ring[i], ring[(i + 1) % n]) for i in range(n)]
    behind = [(b, a) for a, b in ahead]
    outs = [[p] for p in pieces]
    f, b = list(pieces), list(pieces)
    for hop in range(1, n // 2):
        for v in range(2):
            f[v], b[v] = lax.ppermute(f[v], "src", ahead), lax.ppermute(b[v], "src", behind)
            outs[v] += [f[v], b[v]]
        if hop in beside:
            f[0], _ = lax.optimization_barrier((f[0], beside[hop]))
    outs[0].append(lax.ppermute(f[0], "src", ahead))
    outs[1].append(lax.ppermute(b[1], "src", behind))
    return outs


def expand(places, halves, beta_end, scale):
    n = len(halves[0])
    cap, cols = halves[0][0].shape
    batch = beta_end.shape[0]

    def kernel(e_ref, b_ref, s_ref, *refs):
        for which in range(2):

            @pl.when(pl.program_id(0) == which)
            def _(which=which):
                slots = jnp.concatenate([r[...] for r in refs[which * n : (which + 1) * n]], axis=0)
                emitted = jnp.dot(e_ref[...], slots, preferred_element_type=F32)
                refs[-1][...] = (emitted * b_ref[...].astype(F32) * (1.0 / s_ref[...])).astype(BF16)

    return pl.pallas_call(
        kernel,
        grid=(2,),
        in_specs=[
            pl.BlockSpec((batch, n * cap), lambda i: (0, 0)),
            pl.BlockSpec((batch, cols), lambda i: (0, i)),
            pl.BlockSpec((batch, 1), lambda i: (0, 0)),
        ]
        + [pl.BlockSpec((cap, cols), lambda i: (0, 0))] * (2 * n),
        out_specs=pl.BlockSpec((batch, cols), lambda i: (0, i)),
        out_shape=jax.ShapeDtypeStruct(beta_end.shape, BF16),
        **params(4 * batch * n * cap * cols, 4 * cols * (n * cap + 2 * batch)),
    )(places, beta_end, scale, *halves[0], *halves[1])


def counts_chunks(meta, forward, chunks, last, places, transition, counts, factor, tile):
    rows, depth = forward.shape
    n, steps = len(places), len(chunks[0]) + 1
    batch, width = chunks[0][0].shape

    def at(p, m):
        out = m[places[-1]]
        for k in range(n - 1):
            out = jnp.where(p == k, m[places[k]], out)
        return out

    whole = pl.BlockSpec((batch, width), lambda p, i, m: (0, 0))
    in_specs = [
        pl.BlockSpec((tile, depth), lambda p, i, m: (i, 0)),
        pl.BlockSpec((tile, width), lambda p, i, m: (i, at(p, m))),
        pl.BlockSpec((batch, width), lambda p, i, m: (0, at(p, m))),
    ] + [whole] * (n * (steps - 1))

    def kernel(meta_ref, f_ref, t_ref, last_ref, *refs):
        out, stacked = refs[-2:]
        for k in range(n):

            @pl.when((pl.program_id(0) == k) & (pl.program_id(1) == 0))
            def _(k=k):
                for step in range(steps - 1):
                    stacked[pl.ds(step * batch, batch), :] = refs[k * (steps - 1) + step][...]
                stacked[pl.ds((steps - 1) * batch, batch), :] = last_ref[...]

        pairs = jnp.dot(f_ref[...], stacked[...], preferred_element_type=F32)
        out[...] = t_ref[...].astype(F32) * pairs * factor

    args = [forward, transition, last] + [w for chunk in chunks for w in chunk]
    aliases = {}
    if counts is not None:
        in_specs.append(pl.BlockSpec(memory_space=pl.ANY))
        args.append(counts)
        aliases = {len(args): 0}
    return pl.pallas_call(
        kernel,
        grid_spec=pltpu.PrefetchScalarGridSpec(
            num_scalar_prefetch=1,
            grid=(n, rows // tile),
            in_specs=in_specs,
            out_specs=pl.BlockSpec((tile, width), lambda p, i, m: (i, at(p, m))),
            scratch_shapes=[pltpu.VMEM((depth, width), BF16)],
        ),
        out_shape=jax.ShapeDtypeStruct(transition.shape, F32),
        input_output_aliases=aliases,
        **params(2 * rows * depth * width * n, n * (rows * width * 6 + 2 * depth * (rows + width)), COUNTS),
    )(meta, *args)


def capacities(batch, n_src):
    mean = batch // n_src
    return -(-3 * mean // 32) * 16, -(-2 * mean // 16) * 16


def ranks(owner):
    n = owner.shape[0]
    same = owner[:, None] == owner[None, :]
    before = lax.broadcasted_iota(jnp.int32, (n, n), 1) < lax.broadcasted_iota(jnp.int32, (n, n), 0)
    return jnp.sum((same & before).astype(jnp.int32), axis=1)


def slot_plan(caps, transition, emission, forward, beta_end, scales, tokens):
    steps, batch, _ = forward.shape
    src_cols, dst_cols = transition.shape
    n_src, n_dst = lax.axis_size("src"), lax.axis_size("dst")
    n_x, ratio = n_dst // 2, n_src // n_dst
    width = dst_cols // n_src
    words = emission.shape[0]
    s, d = lax.axis_index("src"), lax.axis_index("dst")
    x, core = d // 2, lax.rem(d, 2)
    share = batch // n_dst

    owner = tokens // words
    local = tokens - owner * words
    rest = steps - 1
    cap_a, cap_b = caps
    rank_a = ranks(owner[rest])
    ranks_b = [ranks(owner[step]) for step in range(rest)]

    def word_of_slot(rank, own, loc, cap):
        hit = (rank[None, :] == jnp.arange(cap, dtype=jnp.int32)[:, None]) & (own == s)[None, :]
        return jnp.sum(jnp.where(hit, loc[None, :] + 1, 0), axis=1) - 1

    slot_words = [word_of_slot(rank_a, owner[rest], local[rest], cap_a)]
    slot_words += [word_of_slot(ranks_b[step], owner[step], local[step], cap_b) for step in range(rest)]
    left_half, right_half, *compact_b = compact_rows(
        jnp.concatenate(slot_words), emission, [cap_a] + [cap_b] * rest, width, n_dst
    )

    origin = jnp.asarray(ring_tables(n_src))[s]
    ids = (origin[:, None] * cap_a + jnp.arange(cap_a, dtype=jnp.int32)[None, :]).reshape(-1)
    places_a = ((owner[rest] * cap_a + rank_a)[:, None] == ids[None, :]).astype(BF16)
    flat = forward.reshape(steps * batch, src_cols).T
    slots_a = ring_gather_halves([left_half, right_half], n_src, {1: flat, 2: places_a})
    last = expand(places_a, slots_a, beta_end, scales[rest][:, None])

    def emitted_of(step, tie):
        rows, _ = lax.optimization_barrier((compact_b[step].reshape(n_src, cap_b, width), tie))
        got = lax.all_to_all(rows, "src", 0, 0).reshape(n_src * cap_b, width)
        slot = owner[step] * cap_b + ranks_b[step]
        places = (slot[:, None] == jnp.arange(n_src * cap_b, dtype=jnp.int32)[None, :]).astype(BF16)
        return jnp.dot(places, got, preferred_element_type=BF16)

    to_core = [(t, t ^ 1) for t in range(n_dst)]
    to_x = [(t, (t + 2) % n_dst) for t in range(n_dst)]
    to_part = []
    for a in range(n_src):
        for t in range(n_dst):
            e = (t % 2) * n_x + t // 2
            to_part.append((a * n_dst + t, (e * ratio + a % ratio) * n_dst + a // ratio))

    cols = lax.rem(origin, ratio) * n_dst + origin // ratio
    meta = jnp.concatenate([cols, jnp.stack([core, x]).astype(jnp.int32)])
    core_at, x_at = n_src, n_src + 1
    factor = 32.0 / (steps * batch)
    tiles = src_cols // width

    def from_meta(p):
        return lambda m: m[p]

    def fixed(p):
        return lambda m: p

    def part(h, m):
        return lax.rem(m[x_at] + n_x - 1 - h, n_x)

    def row_there(h, m):
        return (1 - m[core_at]) * n_x + part(h, m)

    def row_here(h, m):
        return m[core_at] * n_x + part(h, m)

    def gathered(pieces, places):
        return [(pieces[p], 0, from_meta(p)) for p in places]

    def between(hop, pieces, done):
        init, counts = done if done is not None else (None, None)
        if hop == 1:
            if len(held) < rest - 1:
                return None
            return None, counts_of([0], pieces, counts)
        new = range(0, 3) if hop == 2 else range(2 * hop - 3, 2 * hop - 1)
        init = product(
            meta, gathered(pieces, new), width, transition, tiles // 2, 2 * width, lambda i, m: i, init
        )
        return init, counts

    def counts_of(places, pieces, counts):
        if not places:
            return counts
        counted.extend(places)
        chunks = [[pieces[p]] + [h[p] for h in held[::-1]] for p in places]
        return counts_chunks(meta, flat, chunks, last, places, transition, counts, factor, src_cols)

    weights, init = [(last, p, fixed(p)) for p in range(n_src)], None
    held, counted = [], []
    for step in range(rest, 0, -1):
        theirs = product(meta, weights, width, transition, n_x, width, row_there, init)
        theirs = lax.ppermute(theirs, "dst", to_core)
        total, emitted = None, None
        for h in range(n_x):
            own = product(
                meta,
                weights,
                width,
                transition,
                2,
                width // 2,
                functools.partial(lambda h, i, m: row_here(h, m) * 2 + i, h),
                init,
            )
            term = own + theirs[:, h * width : (h + 1) * width]
            if total is not None:
                term = term + lax.ppermute(total, "dst", to_x).astype(F32)
            total = term.astype(BF16)
            if emitted is None:
                emitted = emitted_of(step - 1, total)
        message = lax.ppermute(total, ("src", "dst"), to_part)
        mine = (
            emitted.astype(F32) * message.astype(F32) / scales[step - 1][:, None]
        ).astype(BF16)
        pieces, (init, counts) = ring_gather(mine, n_src, between)
        held.append(pieces)
        weights = gathered(pieces, [n_src - 1])

    theirs, own = split_product(meta, weights, width, transition, init, n_x, 2 * width, core_at)
    both = own + lax.ppermute(theirs, "dst", to_core)
    total = None
    for h in range(n_x):
        k = lax.rem(x + n_x - 1 - h, n_x)
        term = lax.dynamic_slice_in_dim(both, k * share, share, 0)
        total = term if total is None else term + lax.ppermute(total, "dst", to_x)
    pieces = held.pop()
    counts = counts_of([p for p in range(n_src) if p not in counted], pieces, counts)
    return counts, total


def per_device(transition, emission, forward, beta_end, scales, tokens):
    steps, batch, _ = forward.shape
    n_src, n_dst = lax.axis_size("src"), lax.axis_size("dst")
    width = transition.shape[1] // n_src
    args = (transition, emission, forward, beta_end, scales, tokens)
    fits = (
        n_src % n_dst == 0
        and n_src & (n_src - 1) == 0
        and n_dst % 2 == 0
        and width % 256 == 0
        and steps > 1
        and (batch // n_dst) % 16 == 0
    )
    if not fits:
        return dense_plan(*args)
    owner = tokens // emission.shape[0]
    held = jnp.sum((owner[:, :, None] == jnp.arange(n_src, dtype=jnp.int32)).astype(jnp.int32), axis=1)
    caps = capacities(batch, n_src)
    room = (jnp.max(held[steps - 1]) <= caps[0]) & (jnp.max(held[: steps - 1]) <= caps[1])
    every = batch, batch
    done = slot_plan(caps, *args)
    return lax.cond(room, lambda done, *_: done, lambda done, *again: slot_plan(every, *again), done, *args)


def solution(mesh):
    in_specs = (P("src", "dst"), P("src", "dst"), P(None, None, "src"), P(None, "dst"), P(), P())
    out_specs = (P("src", "dst"), P("dst", "src"))
    return jax.shard_map(
        per_device, mesh=mesh, in_specs=in_specs, out_specs=out_specs, check_vma=False
    )
```
